32 devices in a mesh: shard: 8 (over z, y), tensor: 4 (over x, core).
Axes of the slice: x: 2, y: 2, z: 4, core: 2. Of those that a mesh axis runs over, the one named last changes fastest.
Arguments:
- grad_parts: float32 [8, 50, 512, 512], P('shard', None, None, 'tensor'), may hold values from -8 to 8
- weights: float32 [50, 512, 512], P(None, 'shard', 'tensor'), may hold values from -0.25 to 0.25
- owner_slot: int32 [50], replicated, may hold values from 0 to 63, as said below
- stat_left: float32 [64, 512, 512], P(('shard', 'tensor')), may hold values from -1 to 5, as said below
- stat_right: float32 [64, 512, 512], P(('shard', 'tensor')), may hold values from -1 to 5, as said below
- root_left: float32 [64, 512, 512], P(('shard', 'tensor')), may hold values from -1 to 5, as said below
- root_right: float32 [64, 512, 512], P(('shard', 'tensor')), may hold values from -1 to 5, as said below
- ln_grad_parts: float32 [8, 4, 1024], P('shard', None, 'tensor'), may hold values from -40 to 40
- ln_params: float32 [4, 1024], P(None, 'tensor'), may hold values from -3 to 3
- ln_accum: float32 [4, 1024], P(None, 'tensor'), may hold values from 0.5 to 5
Outputs:
- new_weights: float32 [50, 512, 512], P(None, 'shard', 'tensor')
- new_stat_left: float32 [64, 512, 512], P(('shard', 'tensor'))
- new_stat_right: float32 [64, 512, 512], P(('shard', 'tensor'))
- new_ln_params: float32 [4, 1024], P(None, 'tensor')
- new_ln_accum: float32 [4, 1024], P(None, 'tensor')
The draws below stay inside these ranges and needn't reach their ends.
Inputs may be any that keep to these rules, and one draw needn't show every extreme that they name: `owner_slot`: distinct global slot numbers; slot s belongs to device s // 2, devices counted with shard slowest. One device owns 2 blocks. `stat_left`: symmetric matrices. `stat_right`: symmetric matrices. `root_left`: symmetric matrices. `root_right`: symmetric matrices.
All inputs are finite; a program needn't handle non-finite values.
Results may differ from the reference program's by a relative error of at most 0.0029.
Values may be sent and summed in bfloat16 or wider, within the bound.
A program may use at most 128 MiB of HBM per device.

```python
import math
import jax
import jax.numpy as jnp
from jax import lax

D = 1024
B = 512
NV = 4
SLOTS = 2
NB = 50
REPLICAS = 8
SLOTS_ALL = 64


def log_uniform(key, shape, lower, upper):
    return jnp.exp(jax.random.uniform(key, shape, jnp.float32, math.log(lower), math.log(upper)))


def symmetric_draw(key, diag_low, diag_high, spread):
    key_diag, key_noise = jax.random.split(key)
    diagonal = log_uniform(key_diag, (SLOTS_ALL, B), diag_low, diag_high)
    noise = jax.random.truncated_normal(key_noise, -4.0, 4.0, (SLOTS_ALL, B, B), jnp.float32)
    noise = (noise + jnp.swapaxes(noise, 1, 2)) * (0.5 * spread / math.sqrt(B))
    return noise + jnp.eye(B, dtype=jnp.float32)[None, :, :] * diagonal[:, :, None]


def draw_stat_left(key, part):
    return symmetric_draw(jax.random.fold_in(key, 31), 0.5, 2.0, 0.9)


def draw_stat_right(key, part):
    return symmetric_draw(jax.random.fold_in(key, 32), 0.5, 2.0, 0.9)


def draw_root_left(key, part):
    return symmetric_draw(jax.random.fold_in(key, 33), 0.5, 2.0, 0.6)


def draw_root_right(key, part):
    return symmetric_draw(jax.random.fold_in(key, 34), 0.5, 2.0, 0.6)


def draw_grad_parts(key, part):
    key_rows, key_cols, key_each = jax.random.split(jax.random.fold_in(key, 41), 3)
    noise = jax.random.truncated_normal(key_each, -4.0, 4.0, (REPLICAS, NB, B, B), jnp.float32)
    row_scale = log_uniform(key_rows, (NB, B, 1), 0.3, 3.0)
    col_scale = log_uniform(key_cols, (NB, 1, B), 0.3, 3.0)
    base = 2.0 / math.sqrt(B) * row_scale * col_scale
    return base[None] * noise / math.sqrt(REPLICAS)


def draw_ln_grad_parts(key, part):
    key_cols, key_each = jax.random.split(jax.random.fold_in(key, 51), 2)
    ramp = 1.0 + 2.0 * jnp.arange(REPLICAS, dtype=jnp.float32) / (REPLICAS - 1)
    col_scale = log_uniform(key_cols, (NV, D), 0.3, 3.0)
    noise = jax.random.truncated_normal(key_each, -4.0, 4.0, (REPLICAS, NV, D), jnp.float32)
    return 0.2 * col_scale[None] * ramp[:, None, None] * noise


def draw_owner_slot(key, part):
    key_busy = jax.random.fold_in(key, 61)
    key_order = jax.random.fold_in(key, 62)
    key_blocks = jax.random.fold_in(key, 63)
    busy_device = jax.random.randint(key_busy, (), 0, SLOTS_ALL // SLOTS)
    scores = jax.random.permutation(key_order, SLOTS_ALL).astype(jnp.int32)
    slot_ids = jnp.arange(SLOTS_ALL, dtype=jnp.int32)
    chosen = slot_ids // SLOTS == busy_device
    scores = jnp.where(chosen, -1 - slot_ids % SLOTS, scores)
    ordering = jnp.argsort(scores, stable=True).astype(jnp.int32)
    picked = ordering[:NB]
    shuffle = jax.random.permutation(key_blocks, NB)
    return picked[shuffle].astype(jnp.int32)


def block_levels(key, extent, cuts, least, top_value):
    level, own = 1.0, jax.random.fold_in(key, 6)
    for position, parts in cuts:
        heights = jnp.exp(jax.random.uniform(jax.random.fold_in(own, position), (parts,), jnp.float32, least / len(cuts), top_value / len(cuts)))
        level = level * jnp.repeat(heights, extent[position] // parts).reshape([-1 if axis == position else 1 for axis in range(len(extent))])
    return level


def scatter_about(stream_key, dims, scale, limit, shards=(), kind=jnp.bfloat16):
    array = jax.random.normal(stream_key, dims, jnp.float32) * scale
    if len(shards) > 0:
        array = block_levels(stream_key, dims, shards, -0.22, 0.18) * array
    return jnp.clip(array, min=-limit, max=limit).astype(kind)


def setup_inputs(seed: int = 0) -> dict:
    keys = jax.random.split(jax.random.key(seed), 11)
    grad_parts = draw_grad_parts(jax.random.fold_in(keys[10], 71), 0)
    weights = scatter_about(keys[1], (NB, B, B), B ** -0.5, 0.25, ((1, 8), (2, 4)), jnp.float32)
    owner_slot = draw_owner_slot(jax.random.fold_in(keys[10], 71), 0)
    stat_left = draw_stat_left(jax.random.fold_in(keys[10], 71), 0)
    stat_right = draw_stat_right(jax.random.fold_in(keys[10], 71), 0)
    root_left = draw_root_left(jax.random.fold_in(keys[10], 71), 0)
    root_right = draw_root_right(jax.random.fold_in(keys[10], 71), 0)
    ln_grad_parts = draw_ln_grad_parts(jax.random.fold_in(keys[10], 71), 0)
    ln_params = scatter_about(keys[8], (NV, D), 0.5, 3.0, ((1, 4),), jnp.float32)
    ln_accum = jnp.clip(jnp.exp(math.log(5.0) - 2.3025851 * jax.random.uniform(keys[9], (NV, D), jnp.float32) ** block_levels(keys[9], (NV, D), ((1, 4),), -0.2, 0.2)), 0.5, 5.0)
    return {"grad_parts": grad_parts, "weights": weights, "owner_slot": owner_slot, "stat_left": stat_left, "stat_right": stat_right, "root_left": root_left, "root_right": root_right, "ln_grad_parts": ln_grad_parts, "ln_params": ln_params, "ln_accum": ln_accum}


DECAY_RATE = 0.9
STEP_RATE = 0.3
NORM_RATE = 0.1
EPSILON = 1e-06
PRECISE = lax.Precision.HIGHEST

def block_step(inputs):
    gradient, stat_lhs, stat_rhs, root_lhs, root_rhs = inputs
    lhs_new = DECAY_RATE * stat_lhs + (1.0 - DECAY_RATE) * jnp.dot(gradient, gradient.T, precision=PRECISE)
    rhs_new = DECAY_RATE * stat_rhs + (1.0 - DECAY_RATE) * jnp.dot(gradient.T, gradient, precision=PRECISE)
    direction = jnp.dot(jnp.dot(root_lhs, gradient, precision=PRECISE), root_rhs, precision=PRECISE)
    factor = jnp.sqrt(jnp.mean(gradient * gradient) / (jnp.mean(direction * direction) + EPSILON))
    update = (STEP_RATE * factor * direction).astype(jnp.bfloat16)
    return (lhs_new, rhs_new, update)

def reference(grad_parts, weights, owner_slot, stat_left, stat_right, root_left, root_right, ln_grad_parts, ln_params, ln_accum):
    gradient = lax.optimization_barrier(jnp.sum(grad_parts, axis=0))
    lhs_new, rhs_new, update = lax.map(block_step, (gradient, stat_left[owner_slot], stat_right[owner_slot], root_left[owner_slot], root_right[owner_slot]))
    new_stat_left = (DECAY_RATE * stat_left).at[owner_slot].set(lhs_new)
    new_stat_right = (DECAY_RATE * stat_right).at[owner_slot].set(rhs_new)
    new_weights = weights - update.astype(jnp.float32)
    ln_gradient = lax.optimization_barrier(jnp.sum(ln_grad_parts, axis=0))
    new_ln_accum = ln_accum + ln_gradient * ln_gradient
    new_ln_params = ln_params - NORM_RATE * ln_gradient / jnp.sqrt(new_ln_accum)
    return (new_weights, new_stat_left, new_stat_right, new_ln_params, new_ln_accum)
```

```python
import jax
import jax.numpy as jnp
from jax import lax
from jax.experimental import pallas as pl
from jax.experimental.pallas import tpu as pltpu
from jax.sharding import PartitionSpec as P

DECAY_RATE = 0.9
STEP_RATE = 0.3
NORM_RATE = 0.1
EPSILON = 1e-06
PRECISE = lax.Precision.HIGHEST
F32 = jnp.float32
BF16 = jnp.bfloat16


def split(value):
    high = value.astype(BF16)
    return high, (value - high.astype(F32)).astype(BF16)


def mul(a, b):
    return jnp.dot(a, b, preferred_element_type=F32)


def mul3(a_high, a_low, b_high, b_low):
    return mul(a_high, b_high) + (mul(a_high, b_low) + mul(a_low, b_high))


def fused_kernel(
    block_of, filled, place_of,
    grad_hbm, weights_ref, stat_l_hbm, stat_r_hbm, root_l_hbm, root_r_hbm, ln_part, ln_params, ln_accum,
    new_w, new_l_hbm, new_r_hbm, new_lnp, new_lna,
    grad, ysend, yrecv, zup, zdown, zsend, total, final, gather, stat_l, stat_r, root_l, root_r,
    g_high, g_low, r_high, r_low, direct, upd, ret, ln_all,
    load_sem, out_sem, ys_sem, yr_sem, zs_sem, zu_sem, zd_sem, gs_sem, gr_sem, us_sem, ur_sem, ls_sem, lr_sem,
):
    side = grad.shape[1]
    width = grad.shape[2]
    sh = lax.axis_index("shard")
    t = lax.axis_index("tensor")
    z, y = sh // 2, sh % 2
    me = sh * 4 + t
    tile = 128
    tiles = side // tile

    def load(src, dst, k):
        return pltpu.make_async_copy(src, dst, load_sem.at[k])

    loads = [
        load(grad_hbm, grad, 0),
        load(root_l_hbm, root_l, 1),
        load(root_r_hbm, root_r, 2),
        load(stat_l_hbm, stat_l, 3),
        load(stat_r_hbm, stat_r, 4),
    ]
    for one in loads:
        one.start()

    def remote(src, dst, send, recv, s, tt):
        return pltpu.make_async_remote_copy(
            src_ref=src, dst_ref=dst, send_sem=send, recv_sem=recv,
            device_id=(s, tt), device_id_type=pl.DeviceIdType.MESH,
        )

    def ln_copy(k):
        return remote(ln_part, ln_all.at[sh], ls_sem.at[k - 1], lr_sem.at[k - 1], lax.rem(sh + k, 8), t)

    for k in range(1, 8):
        ln_copy(k).start()

    def level(c):
        q = lax.rem(c, 4)
        near = 3 - q
        inner = jnp.where(q == 0, 3, jnp.where(q == 1, 0, 4 - q))
        one = jnp.where((z == 0) | (z == 3), near, inner)
        return jnp.where(z < 2, one, 3 - one)

    def unit(n):
        c, td = n // 4, lax.rem(n, 4)
        j, zd = c // 4, level(c)
        return j, zd, td, (j * 4 + zd) * 4 + td

    def slot(j, zd, yd, td):
        return ((zd * 2 + yd) * 4 + td) * 2 + j

    def y_copy(u):
        return remote(ysend.at[u], yrecv.at[u], ys_sem.at[u], yr_sem.at[u], z * 2 + (1 - y), t)

    loads[0].wait()

    def send_y(n, _):
        j, zd, td, u = unit(n)
        s = slot(j, zd, 1 - y, td)
        block, keep = block_of[s], filled[s]

        def rows(i, _):
            r = pl.ds(pl.multiple_of(i * tile, tile), tile)
            ysend[u, r, :] = (grad[block, r, :] * keep).astype(BF16)
            return 0

        lax.fori_loop(0, tiles, rows, 0)
        y_copy(u).start()
        return 0

    lax.fori_loop(0, 32, send_y, 0)

    def up_copy(u):
        return remote(zsend.at[u], zup.at[u], zs_sem.at[u], zu_sem.at[u], jnp.minimum(z + 1, 3) * 2 + y, t)

    def down_copy(u):
        return remote(zsend.at[u], zdown.at[u], zs_sem.at[u], zd_sem.at[u], jnp.maximum(z - 1, 0) * 2 + y, t)

    def gather_copy(j, td):
        return remote(final.at[j, td], gather.at[j, t], gs_sem.at[j, td], gr_sem.at[j, t], sh, td)

    def gather_wait(j, tt):
        return remote(final.at[j, tt], gather.at[j, tt], gs_sem.at[j, tt], gr_sem.at[j, tt], sh, tt)

    def each_tile(body):
        def step(i, _):
            body(pl.ds(pl.multiple_of(i * tile, tile), tile))
            return 0

        lax.fori_loop(0, tiles, step, 0)

    def reduce_unit(n, _):
        j, zd, td, u = unit(n)
        s = slot(j, zd, y, td)
        block, keep = block_of[s], filled[s]
        y_copy(u).wait_recv()

        def first(r):
            total[r, :] = grad[block, r, :] * keep + yrecv[u, r, :].astype(F32)

        each_tile(first)

        @pl.when((z > 0) & (zd >= z))
        def _():
            up_copy(u).wait_recv()

            def add(r):
                total[r, :] = total[r, :] + zup[u, r, :].astype(F32)

            each_tile(add)

        @pl.when((z < 3) & (zd <= z))
        def _():
            down_copy(u).wait_recv()

            def add(r):
                total[r, :] = total[r, :] + zdown[u, r, :].astype(F32)

            each_tile(add)

        @pl.when(zd != z)
        def _():
            def narrow(r):
                zsend[u, r, :] = total[r, :].astype(BF16)

            each_tile(narrow)

        @pl.when(zd > z)
        def _():
            up_copy(u).start()

        @pl.when(zd < z)
        def _():
            down_copy(u).start()

        @pl.when((zd == z) & (td != t))
        def _():
            def keep_sum(r):
                final[j, td, r, :] = total[r, :]

            each_tile(keep_sum)
            gather_copy(j, td).start()

        @pl.when((zd == z) & (td == t))
        def _():
            def keep_own(r):
                gather[j, t, r, :] = total[r, :]

            each_tile(keep_own)

        return 0

    def u_copy(j, k):
        d = lax.rem(me + k, 32)
        s, tt = d // 4, lax.rem(d, 4)
        rows = pl.ds(pl.multiple_of(s * 64, 64), 64)
        return remote(upd.at[j, tt, rows], ret.at[j * 32 + me], us_sem.at[j, k - 1], ur_sem.at[j, k - 1], s, tt)

    def precondition(j):
        for k in range(1, 4):
            gather_wait(j, lax.rem(t + k, 4)).wait_recv()
        cols = [slice(k * width, (k + 1) * width) for k in range(4)]

        def halves(i, sq):
            r = pl.ds(pl.multiple_of(i * tile, tile), tile)
            for k in range(4):
                g = gather[j, k, r, :]
                sq = sq + jnp.sum(g * g, axis=0, keepdims=True)
                g_high[j, r, cols[k]], g_low[r, cols[k]] = split(g)
            r_high[r, :], r_low[r, :] = split(root_r[j, r, :])
            return sq

        zero = jnp.zeros((1, width), F32)
        square = jnp.sum(lax.fori_loop(0, tiles, halves, zero)) * (1.0 / (side * side))

        def product(i, sq):
            r = pl.ds(pl.multiple_of(i * tile, tile), tile)
            half = mul3(*split(root_l[j, r, :]), g_high[j], g_low[...])
            out = mul3(*split(half), r_high[...], r_low[...])
            direct[r, :] = out
            for k in range(4):
                sq = sq + jnp.sum(out[:, cols[k]] * out[:, cols[k]], axis=0, keepdims=True)
            return sq

        mean = jnp.sum(lax.fori_loop(0, tiles, product, zero)) * (1.0 / (side * side))
        ratio = jnp.full((1, width), square, F32) / (jnp.full((1, width), mean, F32) + EPSILON)
        scale = STEP_RATE * jnp.sqrt(ratio)

        def scaled(r):
            for k in range(4):
                upd[j, k, r, :] = (direct[r, cols[k]] * scale).astype(BF16)

        each_tile(scaled)
        own = pl.ds(pl.multiple_of(sh * 64, 64), 64)
        ret[j * 32 + me] = upd[j, t, own, :]

        def start(k, _):
            u_copy(j, k).start()
            return 0

        lax.fori_loop(1, 32, start, 0)

    def statistics(j):
        def left(i, _):
            r = pl.ds(pl.multiple_of(i * tile, tile), tile)
            square = lax.dot_general(
                g_high[j, r, :], g_high[j], (((1,), (1,)), ((), ())), preferred_element_type=F32
            )
            stat_l[j, r, :] = DECAY_RATE * stat_l[j, r, :] + (1.0 - DECAY_RATE) * square
            return 0

        lax.fori_loop(0, tiles, left, 0)

        def right(k, _):
            r = pl.ds(pl.multiple_of(k * width, width), width)
            flipped = gather[j, k].T.astype(BF16)
            stat_r[j, r, :] = DECAY_RATE * stat_r[j, r, :] + (1.0 - DECAY_RATE) * mul(flipped, g_high[j])
            return 0

        lax.fori_loop(0, 4, right, 0)

    lax.fori_loop(0, 20, reduce_unit, 0)
    loads[1].wait()
    loads[2].wait()
    precondition(0)
    lax.fori_loop(20, 32, reduce_unit, 0)
    precondition(1)

    loads[3].wait()
    loads[4].wait()
    statistics(0)
    statistics(1)
    out_l = pltpu.make_async_copy(stat_l, new_l_hbm, out_sem.at[0])
    out_r = pltpu.make_async_copy(stat_r, new_r_hbm, out_sem.at[1])
    out_l.start()
    out_r.start()

    for k in range(1, 8):
        ln_copy(k).wait()
    ln_all[sh] = ln_part[...]
    ln_grad = ln_all[0]
    for k in range(1, 8):
        ln_grad = ln_grad + ln_all[k]
    accum = ln_accum[...] + ln_grad * ln_grad
    new_lna[...] = accum
    new_lnp[...] = ln_params[...] - NORM_RATE * ln_grad / jnp.sqrt(accum)

    def sent(n, _):
        _, zd, _, u = unit(n)
        y_copy(u).wait_send()

        @pl.when(zd != z)
        def _():
            up_copy(u).wait_send()

        return 0

    lax.fori_loop(0, 32, sent, 0)
    for j in range(2):
        for k in range(1, 4):
            gather_copy(j, lax.rem(t + k, 4)).wait_send()

    def landed(n, _):
        u_copy(n // 31, lax.rem(n, 31) + 1).wait()
        return 0

    lax.fori_loop(0, 62, landed, 0)

    def apply(k, _):
        new_w[k] = weights_ref[k] - ret[place_of[k]].astype(F32)
        return 0

    lax.fori_loop(0, weights_ref.shape[0], apply, 0)
    out_l.wait()
    out_r.wait()


def fused(grad_parts, weights, owner_slot, stat_left, stat_right, root_left, root_right, ln_grad_parts, ln_params, ln_accum):
    blocks, side, width = grad_parts.shape[1:]
    slots = 64
    hit = owner_slot[None, :] == jnp.arange(slots, dtype=jnp.int32)[:, None]
    block_of = jnp.sum(jnp.where(hit, jnp.arange(blocks, dtype=jnp.int32)[None, :], 0), axis=1).astype(jnp.int32)
    filled = jnp.any(hit, axis=1).astype(F32)
    place_of = (owner_slot % 2) * 32 + owner_slot // 2
    smem = pl.BlockSpec(memory_space=pltpu.SMEM)
    vmem = pl.BlockSpec(memory_space=pltpu.VMEM)
    hbm = pl.BlockSpec(memory_space=pl.ANY)
    V = pltpu.VMEM
    dma = pltpu.SemaphoreType.DMA
    unit = (32, side, width)
    state = (2, side, side)
    shape = jax.ShapeDtypeStruct
    return pl.pallas_call(
        fused_kernel,
        out_shape=(
            shape(weights.shape, F32), shape(state, F32), shape(state, F32),
            shape(ln_params.shape, F32), shape(ln_params.shape, F32),
        ),
        in_specs=[smem] * 3 + [hbm, vmem] + [hbm] * 4 + [vmem] * 3,
        out_specs=(vmem, hbm, hbm, vmem, vmem),
        scratch_shapes=[
            V((blocks, side, width), F32),
            V(unit, BF16), V(unit, BF16), V(unit, BF16), V(unit, BF16), V(unit, BF16),
            V((side, width), F32),
            V((2, 4, side, width), F32), V((2, 4, side, width), F32),
            V(state, F32), V(state, F32), V(state, F32), V(state, F32),
            V(state, BF16), V((side, side), BF16), V((side, side), BF16), V((side, side), BF16),
            V((side, side), F32),
            V((2, 4, side, width), BF16),
            V((64, 64, width), BF16),
            V((8,) + ln_params.shape, F32),
            dma((5,)), dma((2,)),
            dma((32,)), dma((32,)), dma((32,)), dma((32,)), dma((32,)),
            dma((2, 4)), dma((2, 4)),
            dma((2, 31)), dma((2, 31)),
            dma((7,)), dma((7,)),
        ],
        compiler_params=pltpu.CompilerParams(
            has_side_effects=True, vmem_limit_bytes=60 * 2**20
        ),
        cost_estimate=pl.CostEstimate(flops=2**34, bytes_accessed=2**25, transcendentals=0),
    )(
        block_of, filled, place_of,
        grad_parts[0], weights, stat_left, stat_right, root_left, root_right,
        ln_grad_parts[0], ln_params, ln_accum,
    )


def slot_step(gradient, stat_lhs, stat_rhs, root_lhs, root_rhs):
    lhs_new = DECAY_RATE * stat_lhs + (1.0 - DECAY_RATE) * jnp.dot(
        gradient, gradient.T, precision=PRECISE
    )
    rhs_new = DECAY_RATE * stat_rhs + (1.0 - DECAY_RATE) * jnp.dot(
        gradient.T, gradient, precision=PRECISE
    )
    direction = jnp.dot(jnp.dot(root_lhs, gradient, precision=PRECISE), root_rhs, precision=PRECISE)
    factor = jnp.sqrt(jnp.mean(gradient * gradient) / (jnp.mean(direction * direction) + EPSILON))
    update = (STEP_RATE * factor * direction).astype(jnp.bfloat16)
    return (lhs_new, rhs_new, update)


def apply_kernel(owner_slot, pieces, weights, out):
    def body(k, _):
        out[k] = weights[k] - pieces[owner_slot[k]].astype(F32)
        return 0

    lax.fori_loop(0, weights.shape[0], body, 0)


def general(
    grad_parts, weights, owner_slot, stat_left, stat_right, root_left, root_right, ln_grad_parts, ln_params, ln_accum
):
    shard_count = lax.axis_size("shard")
    tensor_count = lax.axis_size("tensor")
    slot_count = stat_left.shape[0]
    block_side = stat_left.shape[1]
    row_width = block_side // shard_count
    col_width = block_side // tensor_count
    owner_device = owner_slot // slot_count
    slot_place = owner_slot % slot_count
    row_part = lax.psum_scatter(grad_parts[0], "shard", scatter_dimension=1, tiled=True)
    ln_gradient = lax.psum(ln_grad_parts[0], "shard")
    buffer = jnp.zeros((shard_count * tensor_count, slot_count, row_width, col_width), F32)
    buffer = buffer.at[owner_device, slot_place].set(row_part)
    arrived = lax.all_to_all(buffer, ("shard", "tensor"), split_axis=0, concat_axis=0, tiled=True)
    arrived = arrived.reshape(shard_count, tensor_count, slot_count, row_width, col_width)
    owned = arrived.transpose(2, 0, 3, 1, 4).reshape(slot_count, block_side, block_side)
    steps = [
        slot_step(owned[i], stat_left[i], stat_right[i], root_left[i], root_right[i])
        for i in range(slot_count)
    ]
    lhs, rhs, update = (jnp.stack(part) for part in zip(*steps))
    outgoing = update.reshape(slot_count, shard_count, row_width, tensor_count, col_width)
    outgoing = outgoing.transpose(1, 3, 0, 2, 4).reshape(
        shard_count * tensor_count, slot_count, row_width, col_width
    )
    returned = lax.all_to_all(outgoing, ("shard", "tensor"), split_axis=0, concat_axis=0, tiled=True)
    pieces = returned.reshape(-1, row_width, col_width)
    vmem = pl.BlockSpec(memory_space=pltpu.VMEM)
    new_weights = pl.pallas_call(
        apply_kernel,
        out_shape=jax.ShapeDtypeStruct(weights.shape, F32),
        in_specs=[pl.BlockSpec(memory_space=pltpu.SMEM), vmem, vmem],
        out_specs=vmem,
        compiler_params=pltpu.CompilerParams(vmem_limit_bytes=32 * 2**20),
    )(owner_slot, pieces, weights)
    accum = ln_accum + ln_gradient * ln_gradient
    params = ln_params - NORM_RATE * ln_gradient / jnp.sqrt(accum)
    return (new_weights, lhs, rhs, params, accum)


def per_device(*args):
    sizes = (lax.axis_size("shard"), lax.axis_size("tensor"), args[3].shape[0], args[3].shape[1])
    return (fused if sizes == (8, 4, 2, 512) else general)(*args)


def solution(mesh):
    owned = P(("shard", "tensor"), None, None)
    rows = P(None, "shard", "tensor")
    norm = P(None, "tensor")
    return jax.shard_map(
        per_device,
        mesh=mesh,
        in_specs=(
            P("shard", None, None, "tensor"), rows, P(),
            owned, owned, owned, owned, P("shard", None, "tensor"), norm, norm,
        ),
        out_specs=(rows, owned, owned, norm, norm),
        check_vma=False,
    )
```

```python
import jax
import jax.numpy as jnp
from jax import lax
from jax.experimental import pallas as pl
from jax.experimental.pallas import tpu as pltpu
from jax.sharding import PartitionSpec as P

DECAY_RATE = 0.9
STEP_RATE = 0.3
NORM_RATE = 0.1
EPSILON = 1e-06
PRECISE = lax.Precision.HIGHEST
F32 = jnp.float32
BF16 = jnp.bfloat16


def split(value):
    high = value.astype(BF16)
    return high, (value - high.astype(F32)).astype(BF16)


def mul(a, b):
    return jnp.dot(a, b, preferred_element_type=F32)


def mul3(a_high, a_low, b_high, b_low):
    return mul(a_high, b_high) + (mul(a_high, b_low) + mul(a_low, b_high))


def fused_kernel(
    block_of, grad_hbm, root_l_hbm, root_r_hbm, ln_part,
    ret, g_high, ln_sum,
    grad, ysend, yrecv, zup, zdown, zsend, final, gather, root_l, root_r,
    g_low, r_high, r_low, direct, upd, ln_all,
    load_sem, ys_sem, yr_sem, zs_sem, zu_sem, zd_sem, gs_sem, gr_sem, us_sem, ur_sem, ls_sem, lr_sem,
):
    side = grad.shape[1]
    width = grad.shape[2]
    sh = lax.axis_index("shard")
    t = lax.axis_index("tensor")
    z, y = sh // 2, sh % 2
    me = sh * 4 + t
    tile = 128
    tiles = side // tile
    parts = [slice(k * tile, (k + 1) * tile) for k in range(tiles)]

    def load(src, dst, k):
        return pltpu.make_async_copy(src, dst, load_sem.at[k])

    loads = [
        load(grad_hbm, grad, 0),
        load(root_l_hbm, root_l, 1),
        load(root_r_hbm, root_r, 2),
    ]
    for one in loads:
        one.start()

    def remote(src, dst, send, recv, s, tt):
        return pltpu.make_async_remote_copy(
            src_ref=src, dst_ref=dst, send_sem=send, recv_sem=recv,
            device_id=(s, tt), device_id_type=pl.DeviceIdType.MESH,
        )

    def ln_copy(k):
        return remote(ln_part, ln_all.at[sh], ls_sem.at[k - 1], lr_sem.at[k - 1], lax.rem(sh + k, 8), t)

    for k in range(1, 8):
        ln_copy(k).start()

    def level(c):
        q = lax.rem(c, 4)
        near = 3 - q
        inner = jnp.where(q == 0, 3, jnp.where(q == 1, 0, 4 - q))
        one = jnp.where((z == 0) | (z == 3), near, inner)
        return jnp.where(z < 2, one, 3 - one)

    def unit(n):
        k = jnp.maximum(n - 3, 0)
        last = (n >= 3) & ((lax.rem(k, 4) == 3) | (k == 28))
        group = jnp.where(last | (n < 3), k // 4, k // 4 + 1)
        place = jnp.where(last, 3, jnp.where(n < 3, n, lax.rem(k, 4)))
        j, zd = group // 4, level(place)
        td = lax.rem(lax.rem(group, 4) + 1 + t, 4)
        return j, zd, td, (j * 4 + zd) * 4 + td

    def slot(j, zd, yd, td):
        return ((zd * 2 + yd) * 4 + td) * 2 + j

    def found(s):
        block = block_of[s]
        return jnp.maximum(block, 0), jnp.minimum(block + 1, 1).astype(F32)

    def y_copy(u):
        return remote(ysend.at[u], yrecv.at[u], ys_sem.at[u], yr_sem.at[u], z * 2 + (1 - y), t)

    loads[0].wait()

    def send_y(n, _):
        j, zd, td, u = unit(n)
        s = slot(j, zd, 1 - y, td)
        block, keep = found(s)

        for r in parts:
            ysend[u, r, :] = (grad[block, r, :] * keep).astype(BF16)
        y_copy(u).start()
        return 0

    lax.fori_loop(0, 32, send_y, 0)

    def up_copy(u):
        return remote(zsend.at[u], zup.at[u], zs_sem.at[u], zu_sem.at[u], jnp.minimum(z + 1, 3) * 2 + y, t)

    def down_copy(u):
        return remote(zsend.at[u], zdown.at[u], zs_sem.at[u], zd_sem.at[u], jnp.maximum(z - 1, 0) * 2 + y, t)

    def gather_copy(j, td):
        return remote(final.at[j, td], gather.at[j, t], gs_sem.at[j, td], gr_sem.at[j, t], sh, td)

    def gather_wait(j, tt):
        return remote(final.at[j, tt], gather.at[j, tt], gs_sem.at[j, tt], gr_sem.at[j, tt], sh, tt)

    def reduce_unit(n, _):
        j, zd, td, u = unit(n)
        s = slot(j, zd, y, td)
        block, keep = found(s)
        y_copy(u).wait_recv()

        def summed(r, *more):
            value = grad[block, r, :] * keep + yrecv[u, r, :].astype(F32)
            for one in more:
                value = value + one[u, r, :].astype(F32)
            return value

        def pass_on(*more):
            for r in parts:
                zsend[u, r, :] = summed(r, *more).astype(BF16)

        @pl.when(((z == 0) & (zd > 0)) | ((z == 3) & (zd < 3)))
        def _():
            pass_on()

        @pl.when((zd > z) & (z > 0))
        def _():
            up_copy(u).wait_recv()
            pass_on(zup)

        @pl.when((zd < z) & (z < 3))
        def _():
            down_copy(u).wait_recv()
            pass_on(zdown)

        @pl.when(zd > z)
        def _():
            up_copy(u).start()

        @pl.when(zd < z)
        def _():
            down_copy(u).start()

        def finish(*more):
            for r in parts:
                final[j, td, r, :] = summed(r, *more)

        @pl.when((zd == z) & (z == 0))
        def _():
            down_copy(u).wait_recv()
            finish(zdown)

        @pl.when((zd == z) & (z == 3))
        def _():
            up_copy(u).wait_recv()
            finish(zup)

        @pl.when((zd == z) & (z > 0) & (z < 3))
        def _():
            up_copy(u).wait_recv()
            down_copy(u).wait_recv()
            finish(zup, zdown)

        @pl.when((zd == z) & (td != t))
        def _():
            gather_copy(j, td).start()

        @pl.when((zd == z) & (td == t))
        def _():
            for r in parts:
                gather[j, t, r, :] = final[j, td, r, :]

        return 0

    def u_copy(j, k):
        d = lax.rem(me + k, 32)
        s, tt = d // 4, lax.rem(d, 4)
        rows = pl.ds(pl.multiple_of(s * 64, 64), 64)
        return remote(upd.at[j, tt, rows], ret.at[j * 32 + me], us_sem.at[j, k - 1], ur_sem.at[j, k - 1], s, tt)

    def precondition(j):
        for k in range(1, 4):
            gather_wait(j, lax.rem(t + k, 4)).wait_recv()
        cols = [slice(k * width, (k + 1) * width) for k in range(4)]

        sq = jnp.zeros((1, width), F32)
        for r in parts:
            for k in range(4):
                g = gather[j, k, r, :]
                sq = sq + jnp.sum(g * g, axis=0, keepdims=True)
                g_high[j, r, cols[k]], g_low[r, cols[k]] = split(g)
        square = jnp.sum(sq) * (1.0 / (side * side))

        def product(i, sq):
            r = pl.ds(pl.multiple_of(i * 256, 256), 256)
            half = mul3(*split(root_l[j, r, :]), g_high[j], g_low[...])
            out = mul3(*split(half), r_high[j], r_low[j])
            direct[r, :] = out
            for k in range(4):
                sq = sq + jnp.sum(out[:, cols[k]] * out[:, cols[k]], axis=0, keepdims=True)
            return sq

        sq = lax.fori_loop(0, side // 256, product, jnp.zeros((1, width), F32))
        mean = jnp.sum(sq) * (1.0 / (side * side))
        ratio = jnp.full((1, width), square, F32) / (jnp.full((1, width), mean, F32) + EPSILON)
        scale = STEP_RATE * jnp.sqrt(ratio)
        for r in parts:
            for k in range(4):
                upd[j, k, r, :] = (direct[r, cols[k]] * scale).astype(BF16)
        own = pl.ds(pl.multiple_of(sh * 64, 64), 64)
        ret[j * 32 + me] = upd[j, t, own, :]

        def start(k, _):
            u_copy(j, k).start()
            return 0

        lax.fori_loop(1, 32, start, 0)

    loads[1].wait()
    loads[2].wait()

    def split_right(i, _):
        r = pl.ds(pl.multiple_of(i * tile, tile), tile)
        for j in range(2):
            r_high[j, r, :], r_low[j, r, :] = split(root_r[j, r, :])
        return 0

    lax.fori_loop(0, tiles, split_right, 0)
    lax.fori_loop(0, 22, reduce_unit, 0)
    precondition(0)
    lax.fori_loop(22, 32, reduce_unit, 0)
    precondition(1)

    for k in range(1, 8):
        ln_copy(k).wait()
    ln_all[sh] = ln_part[...]
    ln_grad = ln_all[0]
    for k in range(1, 8):
        ln_grad = ln_grad + ln_all[k]
    ln_sum[...] = ln_grad

    def sent(n, _):
        _, zd, _, u = unit(n)
        y_copy(u).wait_send()

        @pl.when(zd != z)
        def _():
            up_copy(u).wait_send()

        return 0

    lax.fori_loop(0, 32, sent, 0)
    for j in range(2):
        for k in range(1, 4):
            gather_copy(j, lax.rem(t + k, 4)).wait_send()

    def landed(n, _):
        u_copy(n // 31, lax.rem(n, 31) + 1).wait()
        return 0

    lax.fori_loop(0, 62, landed, 0)


def closing_kernel(
    owner_slot, pieces, grads, weights, stat_l, stat_r, ln_grad, ln_params, ln_accum,
    new_w, new_l, new_r, new_lnp, new_lna,
):
    step = pl.program_id(0)
    accum = ln_accum[...] + ln_grad[...] * ln_grad[...]
    new_lna[...] = accum
    new_lnp[...] = ln_params[...] - NORM_RATE * ln_grad[...] / jnp.sqrt(accum)
    tile = stat_l.shape[1]
    first = step * weights.shape[0]
    count = owner_slot.shape[0]
    for k in range(weights.shape[0]):
        s = owner_slot[jnp.minimum(first + k, count - 1)]
        new_w[k] = weights[k] - pieces[lax.rem(s, 2) * 32 + s // 2].astype(F32)
    at = pl.ds(pl.multiple_of(lax.rem(step, grads.shape[1] // tile) * tile, tile), tile)
    square = lax.dot_general(grads[0, at, :], grads[0], (((1,), (1,)), ((), ())), preferred_element_type=F32)
    new_l[0] = DECAY_RATE * stat_l[0] + (1.0 - DECAY_RATE) * square
    flipped = grads[0, :, at].astype(F32).T.astype(BF16)
    new_r[0] = DECAY_RATE * stat_r[0] + (1.0 - DECAY_RATE) * mul(flipped, grads[0])


def closing(owner_slot, pieces, grads, weights, stat_left, stat_right, ln_grad, ln_params, ln_accum):
    side = stat_left.shape[1]
    rows = 4
    steps = 2 * rows
    some = pl.BlockSpec((-(-weights.shape[0] // steps),) + weights.shape[1:], lambda i: (i, 0, 0))
    norm = pl.BlockSpec(ln_params.shape, lambda i: (0, 0))
    stat = pl.BlockSpec((1, side // rows, side), lambda i: (i // rows, i % rows, 0))
    return pl.pallas_call(
        closing_kernel,
        grid=(steps,),
        out_shape=tuple(jax.ShapeDtypeStruct(v.shape, F32) for v in (weights, stat_left, stat_right, ln_params, ln_accum)),
        in_specs=[
            pl.BlockSpec(memory_space=pltpu.SMEM),
            pl.BlockSpec(pieces.shape, lambda i: (0, 0, 0)),
            pl.BlockSpec((1, side, side), lambda i: (i // rows, 0, 0)),
            some, stat, stat, norm, norm, norm,
        ],
        out_specs=(some, stat, stat, norm, norm),
        compiler_params=pltpu.CompilerParams(vmem_limit_bytes=60 * 2**20),
    )(owner_slot, pieces, grads, weights, stat_left, stat_right, ln_grad, ln_params, ln_accum)


def fused(grad_parts, weights, owner_slot, stat_left, stat_right, root_left, root_right, ln_grad_parts, ln_params, ln_accum):
    blocks, side, width = grad_parts.shape[1:]
    slots = 64
    hit = owner_slot[None, :] == jnp.arange(slots, dtype=jnp.int32)[:, None]
    block_of = jnp.max(jnp.where(hit, jnp.arange(blocks, dtype=jnp.int32)[None, :], -1), axis=1)
    smem = pl.BlockSpec(memory_space=pltpu.SMEM)
    vmem = pl.BlockSpec(memory_space=pltpu.VMEM)
    hbm = pl.BlockSpec(memory_space=pl.ANY)
    V = pltpu.VMEM
    dma = pltpu.SemaphoreType.DMA
    unit = (32, side, width)
    state = (2, side, side)
    shape = jax.ShapeDtypeStruct
    pieces, grads, ln_grad = pl.pallas_call(
        fused_kernel,
        out_shape=(
            shape((64, 64, width), BF16), shape(state, BF16),
            shape(ln_params.shape, F32),
        ),
        in_specs=[smem] + [hbm] * 3 + [vmem],
        out_specs=(vmem,) * 3,
        scratch_shapes=[
            V((blocks, side, width), F32),
            V(unit, BF16), V(unit, BF16), V(unit, BF16), V(unit, BF16), V(unit, BF16),
            V((2, 4, side, width), F32), V((2, 4, side, width), F32),
            V(state, F32), V(state, F32),
            V((side, side), BF16), V(state, BF16), V(state, BF16),
            V((side, side), F32),
            V((2, 4, side, width), BF16),
            V((8,) + ln_params.shape, F32),
            dma((3,)),
            dma((32,)), dma((32,)), dma((32,)), dma((32,)), dma((32,)),
            dma((2, 4)), dma((2, 4)),
            dma((2, 31)), dma((2, 31)),
            dma((7,)), dma((7,)),
        ],
        compiler_params=pltpu.CompilerParams(
            has_side_effects=True, vmem_limit_bytes=60 * 2**20
        ),
        cost_estimate=pl.CostEstimate(flops=2**34, bytes_accessed=2**25, transcendentals=0),
    )(
        block_of, grad_parts[0], root_left, root_right, ln_grad_parts[0],
    )
    return closing(
        owner_slot, pieces, grads, weights, stat_left, stat_right, ln_grad, ln_params, ln_accum
    )


def slot_step(gradient, stat_lhs, stat_rhs, root_lhs, root_rhs):
    lhs_new = DECAY_RATE * stat_lhs + (1.0 - DECAY_RATE) * jnp.dot(
        gradient, gradient.T, precision=PRECISE
    )
    rhs_new = DECAY_RATE * stat_rhs + (1.0 - DECAY_RATE) * jnp.dot(
        gradient.T, gradient, precision=PRECISE
    )
    direction = jnp.dot(jnp.dot(root_lhs, gradient, precision=PRECISE), root_rhs, precision=PRECISE)
    factor = jnp.sqrt(jnp.mean(gradient * gradient) / (jnp.mean(direction * direction) + EPSILON))
    update = (STEP_RATE * factor * direction).astype(jnp.bfloat16)
    return (lhs_new, rhs_new, update)


def apply_kernel(owner_slot, pieces, weights, out):
    def body(k, _):
        out[k] = weights[k] - pieces[owner_slot[k]].astype(F32)
        return 0

    lax.fori_loop(0, weights.shape[0], body, 0)


def general(
    grad_parts, weights, owner_slot, stat_left, stat_right, root_left, root_right, ln_grad_parts, ln_params, ln_accum
):
    shard_count = lax.axis_size("shard")
    tensor_count = lax.axis_size("tensor")
    slot_count = stat_left.shape[0]
    block_side = stat_left.shape[1]
    row_width = block_side // shard_count
    col_width = block_side // tensor_count
    owner_device = owner_slot // slot_count
    slot_place = owner_slot % slot_count
    row_part = lax.psum_scatter(grad_parts[0], "shard", scatter_dimension=1, tiled=True)
    ln_gradient = lax.psum(ln_grad_parts[0], "shard")
    buffer = jnp.zeros((shard_count * tensor_count, slot_count, row_width, col_width), F32)
    buffer = buffer.at[owner_device, slot_place].set(row_part)
    arrived = lax.all_to_all(buffer, ("shard", "tensor"), split_axis=0, concat_axis=0, tiled=True)
    arrived = arrived.reshape(shard_count, tensor_count, slot_count, row_width, col_width)
    owned = arrived.transpose(2, 0, 3, 1, 4).reshape(slot_count, block_side, block_side)
    steps = [
        slot_step(owned[i], stat_left[i], stat_right[i], root_left[i], root_right[i])
        for i in range(slot_count)
    ]
    lhs, rhs, update = (jnp.stack(part) for part in zip(*steps))
    outgoing = update.reshape(slot_count, shard_count, row_width, tensor_count, col_width)
    outgoing = outgoing.transpose(1, 3, 0, 2, 4).reshape(
        shard_count * tensor_count, slot_count, row_width, col_width
    )
    returned = lax.all_to_all(outgoing, ("shard", "tensor"), split_axis=0, concat_axis=0, tiled=True)
    pieces = returned.reshape(-1, row_width, col_width)
    vmem = pl.BlockSpec(memory_space=pltpu.VMEM)
    new_weights = pl.pallas_call(
        apply_kernel,
        out_shape=jax.ShapeDtypeStruct(weights.shape, F32),
        in_specs=[pl.BlockSpec(memory_space=pltpu.SMEM), vmem, vmem],
        out_specs=vmem,
        compiler_params=pltpu.CompilerParams(vmem_limit_bytes=32 * 2**20),
    )(owner_slot, pieces, weights)
    accum = ln_accum + ln_gradient * ln_gradient
    params = ln_params - NORM_RATE * ln_gradient / jnp.sqrt(accum)
    return (new_weights, lhs, rhs, params, accum)


def per_device(*args):
    sizes = (lax.axis_size("shard"), lax.axis_size("tensor"), args[3].shape[0], args[3].shape[1])
    return (fused if sizes == (8, 4, 2, 512) else general)(*args)


def solution(mesh):
    owned = P(("shard", "tensor"), None, None)
    rows = P(None, "shard", "tensor")
    norm = P(None, "tensor")
    return jax.shard_map(
        per_device,
        mesh=mesh,
        in_specs=(
            P("shard", None, None, "tensor"), rows, P(),
            owned, owned, owned, owned, P("shard", None, "tensor"), norm, norm,
        ),
        out_specs=(rows, owned, owned, norm, norm),
        check_vma=False,
    )
```
